256 devices in a mesh: sub: 2 (over y_lo), col: 32 (over z, y_hi, core), row: 4 (over x).
Axes of the slice: x: 4, y: 4 (y_hi: 2, y_lo: 2; y = y_hi * 2 + y_lo), z: 8, core: 2. Of those that a mesh axis runs over, the one named last changes fastest.
Arguments:
- front_in: float32 [16384, 16384], P(('sub', 'row'), 'col'), as said below
- child_update: float32 [2, 8192, 8192], P('sub', 'row', 'col'), as said below
- child_map: int32 [2, 8192], replicated, may hold values from 0 to 16383, as said below
Outputs:
- front_out: float32 [16384, 16384], P(('sub', 'row'), 'col')
The draws below stay inside these ranges and needn't reach their ends.
Inputs may be any that keep to these rules, and one draw needn't show every extreme that they name: `child_map`: for each child c the map is one to one; it takes the 256 indices of child tile t onto all 256 indices of one parent tile whose number is congruent to t modulo 32. The two children may land on the same parent tiles. `front_in`: in natural order the front is symmetric, each child's update is symmetric, and the assembled front is positive definite. `child_update`: in natural order each child's update is symmetric.
All inputs are finite; a program needn't handle non-finite values.
Results may differ from the reference program's by a relative error of at most 0.0001.
Values sent between devices are 32-bit elements; how exact they have to be, the bound alone decides.
A program may use at most 64 MiB of HBM per device.

```python
import math
import jax
import jax.numpy as jnp
from jax import lax

FRONT_ORDER = 16384
CHILD_ORDER = 8192
TILE_SIZE = 256
PANELS = 2
GROUPS_ROW = 8
GROUPS_COL = 32
GROUPS_CHILD = 4
CLASSES = 32


def natural_order_drawn(count, groups):
    places = jnp.arange(count, dtype=jnp.int32)
    share = count // groups
    local = places % share
    return (local // TILE_SIZE * groups + places // share) * TILE_SIZE + local % TILE_SIZE


def symmetric_sample(key, count, spread, diag_low, diag_high):
    sample = jax.random.normal(key, (count, count), jnp.float32)
    symmetric = (sample + sample.T) * (0.70710678 * spread)
    diagonal = jax.random.uniform(jax.random.fold_in(key, 7), (count,), jnp.float32, diag_low, diag_high) * math.sqrt(FRONT_ORDER)
    positions = jnp.arange(count, dtype=jnp.int32)
    return symmetric.at[positions, positions].set(diagonal)


def draw_front_in(key, part):
    whole = symmetric_sample(key, FRONT_ORDER, 1.0, 6.0, 9.0)
    vector_key = jax.random.fold_in(key, 29)
    common = 2.0 * jax.random.normal(vector_key, (FRONT_ORDER,), jnp.float32)
    whole = whole + common[:, None] * common[None, :]
    row_order = natural_order_drawn(FRONT_ORDER, GROUPS_ROW)
    col_order = natural_order_drawn(FRONT_ORDER, GROUPS_COL)
    return jnp.take(jnp.take(whole, row_order, axis=0), col_order, axis=1)


def draw_child_update(key, part):
    row_order = natural_order_drawn(CHILD_ORDER, GROUPS_CHILD)
    col_order = natural_order_drawn(CHILD_ORDER, GROUPS_COL)
    results = []
    for source in range(2):
        whole = symmetric_sample(jax.random.fold_in(key, 100 + source), CHILD_ORDER, 0.7, -0.3, 0.0)
        results.append(jnp.take(jnp.take(whole, row_order, axis=0), col_order, axis=1))
    return jnp.stack(results, 0)


def draw_child_map(key, part):
    child_tiles = CHILD_ORDER // TILE_SIZE
    per_class = FRONT_ORDER // TILE_SIZE // CLASSES
    class_keys = jax.random.split(jax.random.fold_in(key, 3), 2 * CLASSES)
    shuffled = jax.vmap(lambda single: jax.random.permutation(single, per_class))(class_keys).reshape(2, CLASSES, per_class)
    class_ids = jnp.arange(CLASSES, dtype=jnp.int32)
    first_class = class_ids == 0
    last_class = class_ids == CLASSES - 1
    pinned = jnp.stack([first_class, jnp.logical_or(first_class, last_class)], 0)
    target = jnp.stack([jnp.zeros((CLASSES,), jnp.int32), jnp.where(last_class, per_class - 1, 0).astype(jnp.int32)], 0)
    rotated_all = (shuffled - shuffled[:, :, :1] + target[:, :, None]) % per_class
    rotated = jnp.where(pinned[:, :, None], rotated_all, shuffled)
    tiles = jnp.arange(child_tiles, dtype=jnp.int32)
    residue = tiles % CLASSES
    within = tiles // CLASSES
    parent_tile = residue[None, :] + CLASSES * rotated[:, residue, within]
    offset_keys = jax.random.split(jax.random.fold_in(key, 11), 2 * child_tiles)
    offsets = jax.vmap(lambda single: jax.random.permutation(single, TILE_SIZE))(offset_keys).reshape(2, child_tiles, TILE_SIZE)
    result = parent_tile[:, :, None] * TILE_SIZE + offsets
    return result.reshape(2, CHILD_ORDER).astype(jnp.int32)


def setup_inputs(seed: int = 0) -> dict:
    seeds = jax.random.split(jax.random.key(seed), 4)
    front_in = draw_front_in(jax.random.fold_in(seeds[3], 71), 0)
    child_update = draw_child_update(jax.random.fold_in(seeds[3], 71), 0)
    child_map = draw_child_map(jax.random.fold_in(seeds[3], 71), 0)
    return dict(front_in=front_in, child_update=child_update, child_map=child_map)


def natural_order(count, groups):
    places = jnp.arange(count, dtype=jnp.int32)
    share = count // groups
    local = places % share
    return (local // TILE_SIZE * groups + places // share) * TILE_SIZE + local % TILE_SIZE

def inverse_order(order):
    return jnp.zeros_like(order).at[order].set(jnp.arange(order.shape[0], dtype=jnp.int32))

def reference(front_in, child_update, child_map):
    row_order = natural_order(FRONT_ORDER, GROUPS_ROW)
    col_order = natural_order(FRONT_ORDER, GROUPS_COL)
    front = jnp.take(jnp.take(front_in, inverse_order(row_order), axis=0), inverse_order(col_order), axis=1)
    child_rows = inverse_order(natural_order(CHILD_ORDER, GROUPS_CHILD))
    child_cols = inverse_order(natural_order(CHILD_ORDER, GROUPS_COL))
    for source in range(2):
        update = jnp.take(jnp.take(child_update[source], child_rows, axis=0), child_cols, axis=1)
        target = child_map[source]
        spread = jnp.zeros((CHILD_ORDER, FRONT_ORDER), jnp.float32).at[:, target].set(update)
        front = front.at[target, :].add(spread)
    tile_of_row = jnp.arange(FRONT_ORDER, dtype=jnp.int32) // TILE_SIZE
    for number in range(PANELS):
        lower_end = number * TILE_SIZE
        upper_end = lower_end + TILE_SIZE
        factor = jnp.linalg.cholesky(front[lower_end:upper_end, lower_end:upper_end])
        inverse = lax.linalg.triangular_solve(factor, jnp.eye(TILE_SIZE, dtype=jnp.float32), left_side=True, lower=True)
        product = lax.dot_general(front[:, lower_end:upper_end], inverse, (((1,), (1,)), ((), ())), precision=lax.Precision.HIGHEST)
        tiled_factor = jnp.tile(factor, (FRONT_ORDER // TILE_SIZE, 1))
        panel = jnp.where((tile_of_row < number)[:, None], 0.0, jnp.where((tile_of_row == number)[:, None], tiled_factor, product))
        tail = panel[upper_end:]
        trailing = front[upper_end:, upper_end:] - lax.dot_general(tail, tail, (((1,), (1,)), ((), ())), precision=lax.Precision.HIGHEST)
        front = front.at[:, lower_end:upper_end].set(panel)
        front = front.at[:upper_end, upper_end:].set(0.0)
        front = front.at[upper_end:, upper_end:].set(trailing)
    return jnp.take(jnp.take(front, row_order, axis=0), col_order, axis=1)
```

```python
import functools

import jax
import jax.numpy as jnp
from jax import lax
from jax.experimental import pallas as pl
from jax.experimental.pallas import tpu as pltpu
from jax.sharding import PartitionSpec as P

TILE = 256
HALF = 128
LEAF = 64
MESH = pl.DeviceIdType.MESH
HIGHEST = lax.Precision.HIGHEST
F32 = jnp.float32
BF16 = jnp.bfloat16


def dot(left, right, contract, precision=None):
    return lax.dot_general(
        left, right, (contract, ((), ())), precision=precision, preferred_element_type=F32
    )


def split3(value):
    high = value.astype(BF16)
    rest = value - high.astype(F32)
    mid = rest.astype(BF16)
    low = (rest - mid.astype(F32)).astype(BF16)
    return high, mid, low


def split2(value):
    high = value.astype(BF16)
    return high, (value - high.astype(F32)).astype(BF16)


def permuted(tile, row_of, col_of):
    height, width = row_of.shape[0], col_of.shape[0]
    high, mid, low = split3(tile)
    nt = ((1,), (1,))
    moved = dot(high, col_of, nt) + dot(mid, col_of, nt) + dot(low, col_of, nt)
    high, mid, low = split3(moved)
    nn = ((1,), (0,))
    return dot(row_of, high, nn) + dot(row_of, mid, nn) + dot(row_of, low, nn)


def one_hot(places, count):
    rows = lax.broadcasted_iota(jnp.int32, (count, places.shape[1]), 0)
    return jnp.where(rows == places, 1.0, 0.0).astype(BF16)


def leaf_inverse(block):
    n = block.shape[0]
    rows = lax.broadcasted_iota(jnp.int32, (n, n), 0)
    lanes = lax.broadcasted_iota(jnp.int32, (n, n), 1)
    row_ids = lax.broadcasted_iota(jnp.int32, (n, 1), 0)
    work = block
    for j in range(n - 1):
        column = work[:, j : j + 1]
        row = work[j : j + 1, :]
        pivot = work[j : j + 1, j : j + 1]
        factor = jnp.where(row_ids > j, column * (1.0 / pivot), 0.0)
        changed = work - factor * row
        work = jnp.where(lanes == j, jnp.where(rows > j, -factor, work), changed)
    pivots = jnp.sum(jnp.where(rows == lanes, work, 0.0), axis=1, keepdims=True)
    unit = jnp.where(lanes < rows, work, jnp.where(lanes == rows, 1.0, 0.0))
    return unit * lax.rsqrt(pivots)


def exchange_kernel(
    front_ref, tile_ref, child_ref, row_places_ref, col_places_ref,
    left_ref, right_ref, inverse_ref, child_out_ref,
    made, early, corner, work, strip, send_sems, left_sems, right_sems, inverse_sems,
    child_sems, corner_sems, local_sems,
):
    s = lax.axis_index("sub")
    r = lax.axis_index("row")
    c = lax.axis_index("col")
    z, h, k = c // 4, (c // 2) % 2, c % 2
    g = 4 * s + r

    def col_of(zz, hh, kk):
        return zz * 4 + hh * 2 + kk

    def at(ss=None, rr=None, cc=None):
        return (s if ss is None else ss, c if cc is None else cc, r if rr is None else rr)

    z_up, z_down = (z + 1) % 8, (z + 7) % 8
    to_up = at(cc=col_of(z_up, h, k))
    to_down = at(cc=col_of(z_down, h, k))
    to_far = at(cc=col_of(z, 1 - h, k))
    to_twin = at(cc=col_of(z, h, 1 - k))
    to_sub = at(ss=1 - s)

    def to_row(rr):
        return at(rr=rr)

    barrier = pltpu.get_barrier_semaphore()
    friends = [to_up, to_down, to_far, to_twin, to_sub]
    for step in (1, 2, 3):
        friends.append(at(rr=(r + step) % 4))
        friends.append(at(ss=1 - s, rr=(r + step) % 4))
    for friend in friends:
        pl.semaphore_signal(barrier, inc=1, device_id=friend, device_id_type=MESH)
    pl.semaphore_wait(barrier, len(friends))

    pending = []
    used = [0]

    def slot():
        used[0] += 1
        return send_sems.at[used[0] - 1]

    def send(conditions, source, target, arrive, device):
        copy = pltpu.make_async_remote_copy(
            src_ref=source, dst_ref=target, send_sem=slot(), recv_sem=arrive,
            device_id=device, device_id_type=MESH,
        )
        condition = functools.reduce(jnp.logical_and, conditions)

        @pl.when(condition)
        def _():
            copy.start()

        pending.append((condition, copy))

    def await_at(target, arrive):
        pltpu.make_async_remote_copy(
            src_ref=target, dst_ref=target, send_sem=send_sems.at[0], recv_sem=arrive,
            device_id=to_twin, device_id_type=MESH,
        ).wait_recv()

    always = jnp.bool_(True)
    first = s == 0
    maker = jnp.logical_and(s == 0, r < 2)
    sender_early = jnp.logical_and(s == 1, r < 2)

    send(
        [sender_early],
        child_ref.at[0, pl.ds(0, TILE), :], early, child_sems.at[4], to_sub,
    )

    def send_children(condition):
        for m in range(4):
            place = pl.multiple_of((2 * m + 1 - s) * TILE, TILE)
            send(
                [condition],
                child_ref.at[0, pl.ds(place, TILE), :], child_out_ref.at[m],
                child_sems.at[m], to_sub,
            )

    send_children(jnp.logical_not(maker))

    @pl.when(maker)
    def _():
        await_at(early, child_sems.at[4])
        total = front_ref[...]
        for source in range(2):
            tile = tile_ref[0] if source == 0 else early[...]
            total = total + permuted(
                tile,
                one_hot(row_places_ref[source : source + 1, :], TILE),
                one_hot(col_places_ref[source : source + 1, :], 2 * TILE),
            )
        made[...] = total.reshape(2, HALF, 2 * TILE)

    own_left = c % 8 == g
    left_block = c // 8
    left_group = c % 8
    goal = at(ss=left_group // 4, rr=left_group % 4)
    local_copies = []

    def copy_here(conditions, source, target, number):
        copy = pltpu.make_async_copy(source, target, local_sems.at[number])
        condition = functools.reduce(jnp.logical_and, conditions)

        @pl.when(condition)
        def _():
            copy.start()

        local_copies.append((condition, copy))

    for part in range(2):
        send(
            [first, r == 0, c == 0],
            made.at[part, :, pl.ds(0, TILE)], corner.at[part], corner_sems.at[part],
            at(cc=1),
        )
    for panel in range(2):
        for part in range(2):
            q = 2 * panel + part
            send(
                [first, r == panel, jnp.logical_not(own_left)],
                made.at[part], left_ref.at[left_block, q],
                left_sems.at[left_block, q], goal,
            )
            copy_here(
                [first, r == panel, own_left],
                made.at[part], left_ref.at[left_block, q], q,
            )
            copy_here([first, r == panel], made.at[part], right_ref.at[q], 4 + q)
    for panel in range(2):
        for part in range(2):
            q = 2 * panel + part
            here = [first, r == panel]
            for target in (to_sub, to_row((panel + 1) % 4), to_row((panel + 3) % 4)):
                send(here, made.at[part], right_ref.at[q], right_sems.at[q], target)
    send_children(maker)
    for condition, copy in local_copies:
        pl.when(condition)(copy.wait)

    rides = k == r % 2
    home = h == r // 2
    even = z % 2 == s
    source_rider = jnp.logical_and(rides, even)
    other_rider = jnp.logical_and(rides, jnp.logical_not(even))
    mine = (z // 2) % 4

    def await_left(conditions, m, q):
        condition = functools.reduce(jnp.logical_and, conditions)

        @pl.when(condition)
        def _():
            await_at(left_ref.at[m, q], left_sems.at[m, q])

    def pass_left(conditions, m, q, devices):
        for device in devices:
            send(conditions, left_ref.at[m, q], left_ref.at[m, q], left_sems.at[m, q], device)

    not_made = [
        jnp.logical_not(jnp.logical_and(home, jnp.logical_and(first, r == panel)))
        for panel in range(2)
    ]
    home_source = jnp.logical_and(source_rider, home)
    far_source = jnp.logical_and(source_rider, jnp.logical_not(home))
    for q in range(4):
        await_left([home_source, not_made[q // 2]], mine, q)
        pass_left([home_source], mine, q, [to_far, to_up, to_down, to_twin])

    for panel in range(2):
        near, far, last = (panel + 1) % 4, (panel + 3) % 4, (panel + 2) % 4
        passer = far if panel == 0 else near
        for part in range(2):
            q = 2 * panel + part

            @pl.when(jnp.logical_not(jnp.logical_and(first, r == panel)))
            def _():
                await_at(right_ref.at[q], right_sems.at[q])

            send(
                [jnp.logical_not(first), r == panel],
                right_ref.at[q], right_ref.at[q], right_sems.at[q], to_row(near),
            )
            send(
                [jnp.logical_not(first), r == panel],
                right_ref.at[q], right_ref.at[q], right_sems.at[q], to_row(far),
            )
            send(
                [r == passer],
                right_ref.at[q], right_ref.at[q], right_sems.at[q], to_row(last),
            )

    chief = jnp.logical_and(jnp.logical_and(first, r == 0), c == 1)
    blocks = 2 * TILE // LEAF

    @pl.when(chief)
    def _():
        for part in range(2):
            await_at(corner.at[part], corner_sems.at[part])
        for q in range(4):
            pltpu.make_async_copy(
                right_ref.at[q, :, pl.ds(0, TILE)], strip.at[q], local_sems.at[8 + q]
            ).start()
        for q in range(4):
            pltpu.make_async_copy(
                right_ref.at[q, :, pl.ds(0, TILE)], strip.at[q], local_sems.at[8 + q]
            ).wait()
        work[0:TILE, 0:TILE] = corner[...].reshape(TILE, TILE)
        work[0:TILE, TILE:] = strip[0:2].reshape(TILE, TILE)
        work[TILE:, TILE:] = strip[2:4].reshape(TILE, TILE)
        work[TILE:, 0:TILE] = jnp.zeros((TILE, TILE), F32)

    lanes = lax.broadcasted_iota(jnp.int32, (1, 2 * TILE), 1)
    w_children = [
        ([k == 1], to_twin),
        ([k == 1, z <= 3], to_up),
        ([k == 1, jnp.logical_or(z == 0, z > 5)], to_down),
        ([k == 1, z == 0, h == 0], to_far),
        ([k == 1, z == 0, h == 0, first], to_sub),
        ([k == 1, z == 0, h == 0, first, r == 0], to_row(1)),
        ([k == 1, z == 0, h == 0, first, r == 0], to_row(3)),
        ([k == 1, z == 0, h == 0, first, r == 1], to_row(2)),
    ]

    def send_inverse(b, conditions):
        for more, device in w_children:
            send(
                conditions + more,
                inverse_ref.at[b], inverse_ref.at[b], inverse_sems.at[b], device,
            )

    for b in range(blocks):
        low, high = b * LEAF, (b + 1) * LEAF

        @pl.when(chief)
        def _():
            rows = work[low:high, :]
            leaf = leaf_inverse(rows[:, low:high])
            placed = jnp.concatenate(
                ([jnp.zeros((LEAF, low), F32)] if low else [])
                + [jnp.where(
                    lax.broadcasted_iota(jnp.int32, (LEAF, LEAF), 0)
                    == lax.broadcasted_iota(jnp.int32, (LEAF, LEAF), 1), 1.0, 0.0)]
                + ([jnp.zeros((LEAF, 2 * TILE - high), F32)] if high < 2 * TILE else []),
                axis=1,
            )
            in_block = jnp.logical_and(lanes >= low, lanes < high)
            rows = jnp.where(in_block, placed, rows)
            product = dot(leaf, rows, ((1,), (0,)), HIGHEST)
            made_inverse = jnp.where(lanes < high, product, 0.0)
            early_rows = made_inverse
            work[low:high, :] = early_rows
            if high < 2 * TILE:
                later = product[:, high:]
                below = jnp.where(in_block, 0.0, work[high:, :])
                work[high:, :] = below - dot(later, product, ((0,), (0,)), HIGHEST)
            copy = pltpu.make_async_copy(
                work.at[pl.ds(low, LEAF), :], inverse_ref.at[b], local_sems.at[12]
            )
            copy.start()
            copy.wait()

        send_inverse(b, [chief])

    for q in range(4):
        await_left([far_source], mine, q)
        pass_left([far_source], mine, q, [to_up, to_down, to_twin])
    above, below = (mine + 1) % 4, (mine + 3) % 4
    across = (mine + 2) % 4
    block_down = ((z + 7 - s) // 2) % 4
    block_up = ((z + 1 + 8 - s) // 2) % 4
    for q in range(4):
        await_left([other_rider], block_down, q)
        pass_left([other_rider], block_down, q, [to_up, to_twin])
        await_left([other_rider], block_up, q)
        pass_left([other_rider], block_up, q, [to_down, to_twin])
        await_left([source_rider], below, q)
        pass_left([source_rider], below, q, [to_up, to_twin])
        await_left([source_rider], above, q)
        pass_left([source_rider], above, q, [to_down, to_twin])
    far_down, far_up = (block_down + 3) % 4, (block_up + 1) % 4
    for q in range(4):
        await_left([other_rider], far_down, q)
        pass_left([other_rider], far_down, q, ([to_up] if q < 2 else []) + [to_twin])
        await_left([other_rider], far_up, q)
        pass_left([other_rider], far_up, q, ([to_down] if q >= 2 else []) + [to_twin])
        await_left([source_rider], across, q)
        pass_left([source_rider], across, q, [to_twin])

    for b in range(blocks):
        @pl.when(jnp.logical_not(chief))
        def _():
            await_at(inverse_ref.at[b], inverse_sems.at[b])

        send_inverse(b, [jnp.logical_not(chief)])

    for m in range(4):
        for q in range(4):
            await_left([jnp.logical_not(rides)], m, q)
    for m in range(4):
        await_at(child_out_ref.at[m], child_sems.at[m])
    for condition, copy in pending:
        pl.when(condition)(copy.wait_send)


SENDS = 320


def exchange(front_in, child_update, row_places, col_places):
    blocks = 2 * TILE // LEAF
    outs = (
        jax.ShapeDtypeStruct((4, 4, HALF, 2 * TILE), F32),
        jax.ShapeDtypeStruct((4, HALF, 2 * TILE), F32),
        jax.ShapeDtypeStruct((blocks, LEAF, 2 * TILE), F32),
        jax.ShapeDtypeStruct((4, TILE, TILE), F32),
    )
    return pl.pallas_call(
        exchange_kernel,
        out_shape=outs,
        grid=(1,),
        in_specs=[
            pl.BlockSpec((TILE, 2 * TILE), lambda i: (0, 0)),
            pl.BlockSpec((1, TILE, TILE), lambda i: (0, 0, 0)),
            pl.BlockSpec(memory_space=pl.ANY),
            pl.BlockSpec((2, TILE), lambda i: (0, 0)),
            pl.BlockSpec((2, TILE), lambda i: (0, 0)),
        ],
        out_specs=[pl.BlockSpec(memory_space=pl.ANY)] * 4,
        scratch_shapes=[
            pltpu.VMEM((2, HALF, 2 * TILE), F32),
            pltpu.VMEM((TILE, TILE), F32),
            pltpu.VMEM((2, HALF, TILE), F32),
            pltpu.VMEM((2 * TILE, 2 * TILE), F32),
            pltpu.VMEM((4, HALF, TILE), F32),
            pltpu.SemaphoreType.DMA((SENDS,)),
            pltpu.SemaphoreType.DMA((4, 4)),
            pltpu.SemaphoreType.DMA((4,)),
            pltpu.SemaphoreType.DMA((blocks,)),
            pltpu.SemaphoreType.DMA((5,)),
            pltpu.SemaphoreType.DMA((2,)),
            pltpu.SemaphoreType.DMA((13,)),
        ],
        compiler_params=pltpu.CompilerParams(
            collective_id=0, has_side_effects=True, vmem_limit_bytes=48 * 1024 * 1024
        ),
        name="exchange",
    )(front_in, child_update, child_update, row_places, col_places)


def update_kernel(
    facts_ref, front_ref, mine_ref, other_ref, row_places_ref, col_places_ref,
    left_ref, right_ref, inverse_ref, out_ref, right_high, right_low,
):
    i = pl.program_id(0)
    s, r, c = facts_ref[0], facts_ref[1], facts_ref[2]
    g = 4 * s + r
    number = g + 8 * i
    inverse = inverse_ref[...].reshape(2 * TILE, 2 * TILE)

    @pl.when(i == 0)
    def _():
        done = dot(inverse, right_ref[...].reshape(2 * TILE, 2 * TILE), ((1,), (0,)), HIGHEST)
        high, low = split2(done)
        right_high[...] = high
        right_low[...] = low

    left = left_ref[...].reshape(2 * TILE, TILE)
    done = dot(left, inverse, ((0,), (1,)), HIGHEST)
    high, low = split2(done)
    nn = ((1,), (0,))
    update = (
        dot(high, right_high[...], nn) + dot(high, right_low[...], nn)
        + dot(low, right_high[...], nn)
    )
    out_ref[...] = front_ref[...] - update
    for source in range(2):
        lands = facts_ref[4 + 4 * source + i % 4] == i // 4

        @pl.when(lands)
        def _():
            tile = jnp.where(s == source, mine_ref[0], other_ref[0])
            moved = permuted(
                tile,
                one_hot(row_places_ref[0, source : source + 1, :], TILE),
                one_hot(col_places_ref[source : source + 1, :], TILE),
            )
            place = pl.multiple_of(facts_ref[12 + source] * TILE, TILE)
            out_ref[:, pl.ds(place, TILE)] += moved

    @pl.when(jnp.logical_and(c < 2, number >= 0))
    def _():
        panel = jnp.where(c == 0, done[:, :TILE], done[:, TILE:])
        rows = lax.broadcasted_iota(jnp.int32, (TILE, TILE), 0)
        lanes = lax.broadcasted_iota(jnp.int32, (TILE, TILE), 1)
        keep = jnp.logical_or(number > c, jnp.logical_and(number == c, lanes <= rows))
        out_ref[:, 0:TILE] = jnp.where(keep, panel, 0.0)

    @pl.when(number < 2)
    def _():
        out_ref[:, TILE:] = jnp.zeros((TILE, TILE), F32)

    @pl.when(jnp.logical_and(number < 2, c >= 2))
    def _():
        out_ref[:, 0:TILE] = jnp.zeros((TILE, TILE), F32)


def update(facts, front_in, child_update, arrived, row_places, col_places, left, right, inverse):
    blocks = 2 * TILE // LEAF
    grid_spec = pltpu.PrefetchScalarGridSpec(
        num_scalar_prefetch=1,
        grid=(8,),
        in_specs=[
            pl.BlockSpec((TILE, 2 * TILE), lambda i, f: (i, 0)),
            pl.BlockSpec((1, TILE, TILE), lambda i, f: (0, f[0] + 2 * (i % 4), 0)),
            pl.BlockSpec((1, TILE, TILE), lambda i, f: (i % 4, 0, 0)),
            pl.BlockSpec((1, 2, TILE), lambda i, f: (i % 4, 0, 0)),
            pl.BlockSpec((2, TILE), lambda i, f: (0, 0)),
            pl.BlockSpec((1, 4, HALF, TILE), lambda i, f: (i % 4, 0, 0, i // 4)),
            pl.BlockSpec((4, HALF, 2 * TILE), lambda i, f: (0, 0, 0)),
            pl.BlockSpec((blocks, LEAF, 2 * TILE), lambda i, f: (0, 0, 0)),
        ],
        out_specs=pl.BlockSpec((TILE, 2 * TILE), lambda i, f: (i, 0)),
        scratch_shapes=[
            pltpu.VMEM((2 * TILE, 2 * TILE), BF16),
            pltpu.VMEM((2 * TILE, 2 * TILE), BF16),
        ],
    )
    return pl.pallas_call(
        update_kernel,
        out_shape=jax.ShapeDtypeStruct((8 * TILE, 2 * TILE), F32),
        grid_spec=grid_spec,
        compiler_params=pltpu.CompilerParams(vmem_limit_bytes=48 * 1024 * 1024),
        name="update",
    )(facts, front_in, child_update, arrived, row_places, col_places, left, right, inverse)


def local(front_in, child_update, child_map):
    s = lax.axis_index("sub")
    r = lax.axis_index("row")
    c = lax.axis_index("col")
    g = 4 * s + r
    tiles = child_map.reshape(2, 32, TILE)
    col_map = lax.dynamic_index_in_dim(tiles, c, 1, keepdims=False)
    row_map = lax.dynamic_index_in_dim(tiles.reshape(2, 4, 8, TILE), g, 2, keepdims=False)
    early_rows = row_map[:, 0] - g * TILE
    early_cols = col_map // (32 * TILE) * TILE + col_map % TILE
    left, right, inverse, arrived = exchange(front_in, child_update, early_rows, early_cols)
    facts = jnp.concatenate(
        [
            jnp.stack([s, r, c, 0 * s]).astype(jnp.int32),
            (row_map[:, :, 0] // (32 * TILE)).reshape(-1),
            col_map[:, 0] // (32 * TILE),
        ]
    )
    return update(
        facts, front_in, child_update, arrived,
        jnp.swapaxes(row_map % TILE, 0, 1), col_map % TILE, left, right, inverse,
    )


def solution(mesh):
    placed = (P(("sub", "row"), "col"), P("sub", "row", "col"), P())
    return jax.shard_map(
        local, mesh=mesh, in_specs=placed, out_specs=P(("sub", "row"), "col"), check_vma=False
    )
```

```python
import functools

import jax
import jax.numpy as jnp
from jax import lax
from jax.experimental import pallas as pl
from jax.experimental.pallas import tpu as pltpu
from jax.sharding import PartitionSpec as P

TILE = 256
HALF = 128
LEAF = 64
PARTS = 4
RUN = 2 * TILE // PARTS
MESH = pl.DeviceIdType.MESH
HIGHEST = lax.Precision.HIGHEST
F32 = jnp.float32
BF16 = jnp.bfloat16


def dot(left, right, contract, precision=None):
    return lax.dot_general(
        left, right, (contract, ((), ())), precision=precision, preferred_element_type=F32
    )


def split3(value):
    high = value.astype(BF16)
    rest = value - high.astype(F32)
    mid = rest.astype(BF16)
    low = (rest - mid.astype(F32)).astype(BF16)
    return high, mid, low


def split2(value):
    high = value.astype(BF16)
    return high, (value - high.astype(F32)).astype(BF16)


def dot3(left, right, contract):
    return (
        dot(left[0], right[0], contract) + dot(left[0], right[1], contract)
        + dot(left[1], right[0], contract)
    )


def permuted(tile, row_of, col_of):
    height, width = row_of.shape[0], col_of.shape[0]
    high, mid, low = split3(tile)
    nt = ((1,), (1,))
    moved = dot(high, col_of, nt) + dot(mid, col_of, nt) + dot(low, col_of, nt)
    high, mid, low = split3(moved)
    nn = ((1,), (0,))
    return dot(row_of, high, nn) + dot(row_of, mid, nn) + dot(row_of, low, nn)


def one_hot(places, count):
    rows = lax.broadcasted_iota(jnp.int32, (count, places.shape[1]), 0)
    return jnp.where(rows == places, 1.0, 0.0).astype(BF16)


def leaf_inverse(block):
    n = block.shape[0]
    count = n // 8
    rows = lax.broadcasted_iota(jnp.int32, (8, n), 0)
    lanes = lax.broadcasted_iota(jnp.int32, (8, n), 1)
    slabs = [block[8 * t : 8 * t + 8, :] for t in range(count)]
    for t in range(count):
        base = 8 * t
        spread = [
            [jnp.broadcast_to(slabs[u][:, base + k : base + k + 1], (8, n)) for u in range(t, count)]
            for k in range(8)
        ]
        pivots = None
        for j in range(8):
            pivot = spread[j][0][j : j + 1, :]
            inverse = reciprocal(pivot)
            heads = [spread[k][0][j : j + 1, :] * inverse for k in range(j + 1, 8)]
            scaled = slabs[t][j : j + 1, :] * inverse
            everywhere = jnp.broadcast_to(pivot, (8, n))
            pivots = everywhere if j == 0 else jnp.where(rows == j, everywhere, pivots)
            for u in range(t, count):
                factor = spread[j][u - t]
                if u == t:
                    factor = jnp.where(rows > j, factor, 0.0)
                for k in range(j + 1, 8):
                    spread[k][u - t] = spread[k][u - t] - factor * heads[k - j - 1]
                changed = slabs[u] - factor * scaled
                entry = -(factor * inverse)
                if u == t:
                    entry = jnp.where(rows > j, entry, jnp.where(rows == j, 1.0, slabs[u]))
                slabs[u] = jnp.where(lanes == base + j, entry, changed)
        slabs[t] = slabs[t] * lax.rsqrt(pivots)
    whole = jnp.concatenate(slabs, axis=0)
    rows = lax.broadcasted_iota(jnp.int32, (n, n), 0)
    lanes = lax.broadcasted_iota(jnp.int32, (n, n), 1)
    return jnp.where(lanes <= rows, whole, 0.0)


def reciprocal(value):
    guess = pltpu.reciprocal(value, approx=True)
    return guess * (2.0 - value * guess)


def exchange_kernel(
    front_ref, tile_ref, child_ref, row_places_ref, col_places_ref,
    left_ref, right_ref, inverse_ref, child_out_ref,
    made, turned, early, corner, work, strip, send_sems, left_sems, right_sems, inverse_sems,
    child_sems, corner_sems, local_sems,
):
    s = lax.axis_index("sub")
    r = lax.axis_index("row")
    c = lax.axis_index("col")
    z, h, k = c // 4, (c // 2) % 2, c % 2
    g = 4 * s + r

    def col_of(zz, hh, kk):
        return zz * 4 + hh * 2 + kk

    def at(ss=None, rr=None, cc=None):
        return (s if ss is None else ss, c if cc is None else cc, r if rr is None else rr)

    z_up, z_down = (z + 1) % 8, (z + 7) % 8
    to_up = at(cc=col_of(z_up, h, k))
    to_down = at(cc=col_of(z_down, h, k))
    to_far = at(cc=col_of(z, 1 - h, k))
    to_twin = at(cc=col_of(z, h, 1 - k))
    to_sub = at(ss=1 - s)

    def to_row(rr):
        return at(rr=rr)

    barrier = pltpu.get_barrier_semaphore()
    friends = [to_up, to_down, to_far, to_twin, to_sub]
    for step in (1, 2, 3):
        friends.append(at(rr=(r + step) % 4))
        friends.append(at(ss=1 - s, rr=(r + step) % 4))
        friends.append(at(rr=(r + step) % 4, cc=col_of(z, 1 - h, k)))
        friends.append(at(ss=1 - s, rr=(r + step) % 4, cc=col_of(z, 1 - h, k)))
    friends.append(at(ss=1 - s, cc=col_of(z, 1 - h, k)))
    for friend in friends:
        pl.semaphore_signal(barrier, inc=1, device_id=friend, device_id_type=MESH)
    pl.semaphore_wait(barrier, len(friends))

    pending = []
    used = [0]

    def slot():
        used[0] += 1
        return send_sems.at[used[0] - 1]

    def send(conditions, source, target, arrive, device):
        copy = pltpu.make_async_remote_copy(
            src_ref=source, dst_ref=target, send_sem=slot(), recv_sem=arrive,
            device_id=device, device_id_type=MESH,
        )
        condition = functools.reduce(jnp.logical_and, conditions)

        @pl.when(condition)
        def _():
            copy.start()

        pending.append((condition, copy))

    def await_at(target, arrive):
        pltpu.make_async_remote_copy(
            src_ref=target, dst_ref=target, send_sem=send_sems.at[0], recv_sem=arrive,
            device_id=to_twin, device_id_type=MESH,
        ).wait_recv()

    always = jnp.bool_(True)
    first = s == 0
    maker = jnp.logical_and(s == 0, r < 2)
    sender_early = jnp.logical_and(s == 1, r < 2)

    send(
        [sender_early],
        child_ref.at[0, pl.ds(0, TILE), :], early, child_sems.at[4], to_sub,
    )

    def send_children(numbers):
        for m in numbers:
            place = pl.multiple_of((2 * m + 1 - s) * TILE, TILE)
            send(
                [always],
                child_ref.at[0, pl.ds(place, TILE), :], child_out_ref.at[m],
                child_sems.at[m], to_sub,
            )

    send_children((0, 1))

    @pl.when(maker)
    def _():
        await_at(early, child_sems.at[4])
        total = front_ref[...]
        for source in range(2):
            tile = tile_ref[0] if source == 0 else early[...]
            total = total + permuted(
                tile,
                one_hot(row_places_ref[source : source + 1, :], TILE),
                one_hot(col_places_ref[source : source + 1, :], 2 * TILE),
            )
        made[...] = total.reshape(2, HALF, 2 * TILE)
        turned[...] = total.T

    own_left = c % 8 == g
    left_block = c // 8
    left_group = c % 8
    goal = at(ss=left_group // 4, rr=left_group % 4)
    far_goal = at(ss=left_group // 4, rr=left_group % 4, cc=col_of(z, 1 - h, k))
    local_copies = []

    def copy_here(conditions, source, target, number):
        copy = pltpu.make_async_copy(source, target, local_sems.at[number])
        condition = functools.reduce(jnp.logical_and, conditions)

        @pl.when(condition)
        def _():
            copy.start()

        local_copies.append((condition, copy))

    for part in range(2):
        send(
            [first, r == 0, c == 0],
            made.at[part, :, pl.ds(0, TILE)], corner.at[part], corner_sems.at[part],
            at(cc=1),
        )
    def left_at(m, q):
        return left_ref.at[m, q // PARTS, pl.ds(q % PARTS * RUN, RUN), :]

    for panel in range(2):
        here = [first, r == panel]
        for part in range(PARTS):
            q = PARTS * panel + part
            piece = turned.at[pl.ds(part * RUN, RUN), :]
            send(
                here + [jnp.logical_not(own_left)],
                piece, left_at(left_block, q), left_sems.at[left_block, q], goal,
            )
            send(here, piece, left_at(left_block, q), left_sems.at[left_block, q], far_goal)
        copy_here(here + [own_left], turned, left_ref.at[left_block, panel], panel)
        copy_here(here, made, right_ref.at[pl.ds(2 * panel, 2)], 4 + panel)
    for panel in range(2):
        for part in range(2):
            q = 2 * panel + part
            here = [first, r == panel]
            for target in (to_sub, to_row((panel + 1) % 4), to_row((panel + 3) % 4)):
                send(here, made.at[part], right_ref.at[q], right_sems.at[q], target)
    for condition, copy in local_copies:
        pl.when(condition)(copy.wait)

    rides = k == r % 2
    home = h == r // 2
    even = z % 2 == s
    source_rider = jnp.logical_and(rides, even)
    other_rider = jnp.logical_and(rides, jnp.logical_not(even))
    mine = (z // 2) % 4

    def await_left(conditions, m, q):
        condition = functools.reduce(jnp.logical_and, conditions)

        @pl.when(condition)
        def _():
            await_at(left_at(m, q), left_sems.at[m, q])

    def pass_left(conditions, m, q, devices):
        for device in devices:
            send(conditions, left_at(m, q), left_at(m, q), left_sems.at[m, q], device)

    not_made = [
        jnp.logical_not(jnp.logical_and(home, jnp.logical_and(first, r == panel)))
        for panel in range(2)
    ]
    for q in range(2 * PARTS):
        await_left([source_rider, not_made[q // PARTS]], mine, q)
        pass_left([source_rider], mine, q, [to_up, to_down, to_twin])

    def pass_right(who):
        for panel in range(2):
            near, far, last = (panel + 1) % 4, (panel + 3) % 4, (panel + 2) % 4
            passer = far if panel == 0 else near
            for part in range(2):
                q = 2 * panel + part
                turn = jnp.logical_and(jnp.logical_not(first), r == panel)
                passes = jnp.logical_and(who, jnp.logical_or(turn, r == passer))

                @pl.when(passes)
                def _():
                    await_at(right_ref.at[q], right_sems.at[q])

                for condition, target in ((turn, near), (turn, far), (r == passer, last)):
                    send(
                        [who, condition],
                        right_ref.at[q], right_ref.at[q], right_sems.at[q], to_row(target),
                    )

    def await_right(who):
        for panel in range(2):
            passer = (panel + 3) % 4 if panel == 0 else (panel + 1) % 4
            for part in range(2):
                q = 2 * panel + part
                done = jnp.logical_or(r == panel, r == passer)

                @pl.when(jnp.logical_and(who, jnp.logical_not(done)))
                def _():
                    await_at(right_ref.at[q], right_sems.at[q])

    pass_right(jnp.logical_not(rides))

    chief = jnp.logical_and(jnp.logical_and(first, r == 0), c == 1)
    blocks = 2 * TILE // LEAF

    @pl.when(chief)
    def _():
        for part in range(2):
            await_at(corner.at[part], corner_sems.at[part])
            await_at(right_ref.at[2 + part], right_sems.at[2 + part])
        for q in range(4):
            pltpu.make_async_copy(
                right_ref.at[q, :, pl.ds(0, TILE)], strip.at[q], local_sems.at[8 + q]
            ).start()
        for q in range(4):
            pltpu.make_async_copy(
                right_ref.at[q, :, pl.ds(0, TILE)], strip.at[q], local_sems.at[8 + q]
            ).wait()
        work[0:TILE, 0:TILE] = corner[...].reshape(TILE, TILE)
        work[0:TILE, TILE:] = strip[0:2].reshape(TILE, TILE)
        work[TILE:, TILE:] = strip[2:4].reshape(TILE, TILE)
        work[TILE:, 0:TILE] = jnp.zeros((TILE, TILE), F32)

    lanes = lax.broadcasted_iota(jnp.int32, (1, 2 * TILE), 1)
    w_children = [
        ([k == 1], to_twin),
        ([k == 1, r == 0], to_row(1)),
        ([k == 1, r == 0], to_row(3)),
        ([k == 1, r == 1], to_row(2)),
        ([k == 1, r == 0, first], to_sub),
        ([k == 1, r == 0, first, h == 0], to_far),
        ([k == 1, r == 0, first, h == 0, z <= 3], to_up),
        ([k == 1, r == 0, first, h == 0, jnp.logical_or(z == 0, z > 5)], to_down),
    ][::-1]

    def inverse_at(b):
        reach = ((b + 1) * LEAF + HALF - 1) // HALF * HALF
        return inverse_ref.at[b, :, pl.ds(0, reach)]

    def send_inverse(b, conditions):
        for more, device in w_children:
            send(
                conditions + more,
                inverse_at(b), inverse_at(b), inverse_sems.at[b], device,
            )

    for b in range(blocks):
        low, high = b * LEAF, (b + 1) * LEAF

        @pl.when(chief)
        def _():
            rows = work[low:high, :]
            leaf = leaf_inverse(rows[:, low:high])
            placed = jnp.concatenate(
                ([jnp.zeros((LEAF, low), F32)] if low else [])
                + [jnp.where(
                    lax.broadcasted_iota(jnp.int32, (LEAF, LEAF), 0)
                    == lax.broadcasted_iota(jnp.int32, (LEAF, LEAF), 1), 1.0, 0.0)]
                + ([jnp.zeros((LEAF, 2 * TILE - high), F32)] if high < 2 * TILE else []),
                axis=1,
            )
            in_block = jnp.logical_and(lanes >= low, lanes < high)
            rows = jnp.where(in_block, placed, rows)
            product = dot(leaf, rows, ((1,), (0,)), HIGHEST)
            made_inverse = jnp.where(lanes < high, product, 0.0)
            early_rows = made_inverse
            work[low:high, :] = early_rows
            if high < 2 * TILE:
                later = product[:, high:]
                below = jnp.where(in_block, 0.0, work[high:, :])
                work[high:, :] = below - dot(later, product, ((0,), (0,)), HIGHEST)
            copy = pltpu.make_async_copy(
                work.at[pl.ds(low, LEAF), :], inverse_ref.at[b], local_sems.at[12]
            )
            copy.start()
            copy.wait()

        send_inverse(b, [chief])

    above, below = (mine + 1) % 4, (mine + 3) % 4
    across = (mine + 2) % 4
    block_down = ((z + 7 - s) // 2) % 4
    block_up = ((z + 1 + 8 - s) // 2) % 4
    for q in range(2 * PARTS):
        await_left([other_rider], block_down, q)
        pass_left([other_rider], block_down, q, [to_up, to_twin])
        await_left([other_rider], block_up, q)
        pass_left([other_rider], block_up, q, [to_down, to_twin])
        await_left([source_rider], below, q)
        pass_left([source_rider], below, q, [to_up, to_twin])
        await_left([source_rider], above, q)
        pass_left([source_rider], above, q, [to_down, to_twin])
    pass_right(rides)
    send_children((2, 3))
    far_down, far_up = (block_down + 3) % 4, (block_up + 1) % 4
    for q in range(2 * PARTS):
        await_left([other_rider], far_down, q)
        pass_left([other_rider], far_down, q, ([to_up] if q < PARTS else []) + [to_twin])
        await_left([other_rider], far_up, q)
        pass_left([other_rider], far_up, q, ([to_down] if q >= PARTS else []) + [to_twin])
        await_left([source_rider], across, q)
        pass_left([source_rider], across, q, [to_twin])

    for b in range(blocks):
        @pl.when(jnp.logical_not(chief))
        def _():
            await_at(inverse_at(b), inverse_sems.at[b])

        send_inverse(b, [jnp.logical_not(chief)])

    await_right(jnp.logical_not(chief))
    for m in range(4):
        for q in range(2 * PARTS):
            await_left([jnp.logical_not(rides)], m, q)
    for m in range(4):
        await_at(child_out_ref.at[m], child_sems.at[m])
    for condition, copy in pending:
        pl.when(condition)(copy.wait_send)


SENDS = 400


def exchange(front_in, child_update, row_places, col_places):
    blocks = 2 * TILE // LEAF
    outs = (
        jax.ShapeDtypeStruct((4, 2, 2 * TILE, TILE), F32),
        jax.ShapeDtypeStruct((4, HALF, 2 * TILE), F32),
        jax.ShapeDtypeStruct((blocks, LEAF, 2 * TILE), F32),
        jax.ShapeDtypeStruct((4, TILE, TILE), F32),
    )
    return pl.pallas_call(
        exchange_kernel,
        out_shape=outs,
        grid=(1,),
        in_specs=[
            pl.BlockSpec((TILE, 2 * TILE), lambda i: (0, 0)),
            pl.BlockSpec((1, TILE, TILE), lambda i: (0, 0, 0)),
            pl.BlockSpec(memory_space=pl.ANY),
            pl.BlockSpec((2, TILE), lambda i: (0, 0)),
            pl.BlockSpec((2, TILE), lambda i: (0, 0)),
        ],
        out_specs=[pl.BlockSpec(memory_space=pl.ANY)] * 4,
        scratch_shapes=[
            pltpu.VMEM((2, HALF, 2 * TILE), F32),
            pltpu.VMEM((2 * TILE, TILE), F32),
            pltpu.VMEM((TILE, TILE), F32),
            pltpu.VMEM((2, HALF, TILE), F32),
            pltpu.VMEM((2 * TILE, 2 * TILE), F32),
            pltpu.VMEM((4, HALF, TILE), F32),
            pltpu.SemaphoreType.DMA((SENDS,)),
            pltpu.SemaphoreType.DMA((4, 2 * PARTS)),
            pltpu.SemaphoreType.DMA((4,)),
            pltpu.SemaphoreType.DMA((blocks,)),
            pltpu.SemaphoreType.DMA((5,)),
            pltpu.SemaphoreType.DMA((2,)),
            pltpu.SemaphoreType.DMA((13,)),
        ],
        compiler_params=pltpu.CompilerParams(
            collective_id=0, has_side_effects=True, vmem_limit_bytes=48 * 1024 * 1024
        ),
        name="exchange",
    )(front_in, child_update, child_update, row_places, col_places)


def update_kernel(
    facts_ref, front_ref, mine_ref, other_ref, row_places_ref, col_places_ref,
    left_ref, right_ref, inverse_ref, out_ref, w_high, w_low, right_high, right_low,
):
    m = pl.program_id(0)
    s, r, c = facts_ref[0], facts_ref[1], facts_ref[2]
    g = 4 * s + r
    nn, nt = ((1,), (0,)), ((1,), (1,))

    def half_of(ref_high, ref_low, row, col):
        rows, cols = pl.ds(row * TILE, TILE), pl.ds(col * TILE, TILE)
        return ref_high[rows, cols], ref_low[rows, cols]

    @pl.when(m == 0)
    def _():
        rows = lax.broadcasted_iota(jnp.int32, (2 * TILE, 2 * TILE), 0)
        lanes = lax.broadcasted_iota(jnp.int32, (2 * TILE, 2 * TILE), 1)
        inverse = inverse_ref[...].reshape(2 * TILE, 2 * TILE)
        w_high[...], w_low[...] = split2(jnp.where(lanes <= rows, inverse, 0.0))
        high, low = split2(right_ref[...].reshape(2 * TILE, 2 * TILE))
        upper = dot3(half_of(w_high, w_low, 0, 0), (high[:TILE], low[:TILE]), nn)
        lower = dot3((w_high[TILE:], w_low[TILE:]), (high, low), nn)
        right_high[:TILE], right_low[:TILE] = split2(upper)
        right_high[TILE:], right_low[TILE:] = split2(lower)

    first, second = split2(left_ref[0, 0]), split2(left_ref[0, 1])
    done = (
        dot3(first, half_of(w_high, w_low, 0, 0), nt),
        dot3(first, half_of(w_high, w_low, 1, 0), nt)
        + dot3(second, half_of(w_high, w_low, 1, 1), nt),
    )
    total = None
    for part in range(2):
        rows = pl.ds(part * TILE, TILE)
        product = dot3(split2(done[part]), (right_high[rows, :], right_low[rows, :]), nn)
        total = product if total is None else total + product
    for half in range(2):
        out_ref[half, 0] = front_ref[half, 0] - total[half * TILE : (half + 1) * TILE]
    for source in range(2):
        tile = jnp.where(s == source, mine_ref[0], other_ref[0])
        moved = permuted(
            tile,
            one_hot(row_places_ref[0, source : source + 1, :], TILE),
            one_hot(col_places_ref[source : source + 1, :], TILE),
        )
        half = facts_ref[4 + 4 * source + m]
        place = pl.multiple_of(facts_ref[12 + source] * TILE, TILE)
        out_ref[half, 0, :, pl.ds(place, TILE)] += moved

    @pl.when(c < 2)
    def _():
        rows = lax.broadcasted_iota(jnp.int32, (TILE, TILE), 0)
        lanes = lax.broadcasted_iota(jnp.int32, (TILE, TILE), 1)
        for half in range(2):
            number = g + 8 * m + 32 * half
            cut = slice(half * TILE, (half + 1) * TILE)
            panel = jnp.where(c == 0, done[0][cut], done[1][cut])
            keep = jnp.logical_or(number > c, jnp.logical_and(number == c, lanes <= rows))
            out_ref[half, 0, :, 0:TILE] = jnp.where(keep, panel, 0.0)

    @pl.when(jnp.logical_and(m == 0, g < 2))
    def _():
        out_ref[0, 0, :, TILE:] = jnp.zeros((TILE, TILE), F32)

    @pl.when(jnp.logical_and(jnp.logical_and(m == 0, g < 2), c >= 2))
    def _():
        out_ref[0, 0, :, 0:TILE] = jnp.zeros((TILE, TILE), F32)


def update(facts, front_in, child_update, arrived, row_places, col_places, left, right, inverse):
    blocks = 2 * TILE // LEAF
    grid_spec = pltpu.PrefetchScalarGridSpec(
        num_scalar_prefetch=1,
        grid=(4,),
        in_specs=[
            pl.BlockSpec((2, 1, TILE, 2 * TILE), lambda m, f: (0, m, 0, 0)),
            pl.BlockSpec((1, TILE, TILE), lambda m, f: (0, f[0] + 2 * m, 0)),
            pl.BlockSpec((1, TILE, TILE), lambda m, f: (m, 0, 0)),
            pl.BlockSpec((1, 2, TILE), lambda m, f: (m, 0, 0)),
            pl.BlockSpec((2, TILE), lambda m, f: (0, 0)),
            pl.BlockSpec((1, 2, 2 * TILE, TILE), lambda m, f: (m, 0, 0, 0)),
            pl.BlockSpec((4, HALF, 2 * TILE), lambda m, f: (0, 0, 0)),
            pl.BlockSpec((blocks, LEAF, 2 * TILE), lambda m, f: (0, 0, 0)),
        ],
        out_specs=pl.BlockSpec((2, 1, TILE, 2 * TILE), lambda m, f: (0, m, 0, 0)),
        scratch_shapes=[pltpu.VMEM((2 * TILE, 2 * TILE), BF16)] * 4,
    )
    out = pl.pallas_call(
        update_kernel,
        out_shape=jax.ShapeDtypeStruct((2, 4, TILE, 2 * TILE), F32),
        grid_spec=grid_spec,
        compiler_params=pltpu.CompilerParams(vmem_limit_bytes=48 * 1024 * 1024),
        name="update",
    )(
        facts, front_in.reshape(2, 4, TILE, 2 * TILE), child_update, arrived,
        row_places, col_places, left, right, inverse,
    )
    return out.reshape(8 * TILE, 2 * TILE)


def local(front_in, child_update, child_map):
    s = lax.axis_index("sub")
    r = lax.axis_index("row")
    c = lax.axis_index("col")
    g = 4 * s + r
    tiles = child_map.reshape(2, 32, TILE)
    col_map = lax.dynamic_index_in_dim(tiles, c, 1, keepdims=False)
    row_map = lax.dynamic_index_in_dim(tiles.reshape(2, 4, 8, TILE), g, 2, keepdims=False)
    early_rows = row_map[:, 0] - g * TILE
    early_cols = col_map // (32 * TILE) * TILE + col_map % TILE
    left, right, inverse, arrived = exchange(front_in, child_update, early_rows, early_cols)
    facts = jnp.concatenate(
        [
            jnp.stack([s, r, c, 0 * s]).astype(jnp.int32),
            (row_map[:, :, 0] // (32 * TILE)).reshape(-1),
            col_map[:, 0] // (32 * TILE),
        ]
    )
    return update(
        facts, front_in, child_update, arrived,
        jnp.swapaxes(row_map % TILE, 0, 1), col_map % TILE, left, right, inverse,
    )


def solution(mesh):
    placed = (P(("sub", "row"), "col"), P("sub", "row", "col"), P())
    return jax.shard_map(
        local, mesh=mesh, in_specs=placed, out_specs=P(("sub", "row"), "col"), check_vma=False
    )
```

```python
import functools

import jax
import jax.numpy as jnp
from jax import lax
from jax.experimental import pallas as pl
from jax.experimental.pallas import tpu as pltpu
from jax.sharding import PartitionSpec as P

TILE = 256
HALF = 128
LEAF = 64
PARTS = 4
RUN = 2 * TILE // PARTS
MESH = pl.DeviceIdType.MESH
HIGHEST = lax.Precision.HIGHEST
F32 = jnp.float32
BF16 = jnp.bfloat16


def dot(left, right, contract, precision=None):
    return lax.dot_general(
        left, right, (contract, ((), ())), precision=precision, preferred_element_type=F32
    )


def split3(value):
    high = value.astype(BF16)
    rest = value - high.astype(F32)
    mid = rest.astype(BF16)
    low = (rest - mid.astype(F32)).astype(BF16)
    return high, mid, low


def split2(value):
    high = value.astype(BF16)
    return high, (value - high.astype(F32)).astype(BF16)


def dot3(left, right, contract):
    return (
        dot(left[0], right[0], contract) + dot(left[0], right[1], contract)
        + dot(left[1], right[0], contract)
    )


def permuted(tile, row_of, col_of):
    height, width = row_of.shape[0], col_of.shape[0]
    high, mid, low = split3(tile)
    nt = ((1,), (1,))
    moved = dot(high, col_of, nt) + dot(mid, col_of, nt) + dot(low, col_of, nt)
    high, mid, low = split3(moved)
    nn = ((1,), (0,))
    return dot(row_of, high, nn) + dot(row_of, mid, nn) + dot(row_of, low, nn)


def one_hot(places, count):
    rows = lax.broadcasted_iota(jnp.int32, (count, places.shape[1]), 0)
    return jnp.where(rows == places, 1.0, 0.0).astype(BF16)


def leaf_inverse(block):
    n = block.shape[0]
    count = n // 8
    rows = lax.broadcasted_iota(jnp.int32, (8, n), 0)
    lanes = lax.broadcasted_iota(jnp.int32, (8, n), 1)
    slabs = [block[8 * t : 8 * t + 8, :] for t in range(count)]
    for t in range(count):
        base = 8 * t
        spread = [
            [jnp.broadcast_to(slabs[u][:, base + k : base + k + 1], (8, n)) for u in range(t, count)]
            for k in range(8)
        ]
        pivots = None
        for j in range(8):
            pivot = spread[j][0][j : j + 1, :]
            inverse = reciprocal(pivot)
            heads = [spread[k][0][j : j + 1, :] * inverse for k in range(j + 1, 8)]
            scaled = slabs[t][j : j + 1, :] * inverse
            everywhere = jnp.broadcast_to(pivot, (8, n))
            pivots = everywhere if j == 0 else jnp.where(rows == j, everywhere, pivots)
            for u in range(t, count):
                factor = spread[j][u - t]
                if u == t:
                    factor = jnp.where(rows > j, factor, 0.0)
                for k in range(j + 1, 8):
                    spread[k][u - t] = spread[k][u - t] - factor * heads[k - j - 1]
                changed = slabs[u] - factor * scaled
                entry = -(factor * inverse)
                if u == t:
                    entry = jnp.where(rows > j, entry, jnp.where(rows == j, 1.0, slabs[u]))
                slabs[u] = jnp.where(lanes == base + j, entry, changed)
        slabs[t] = slabs[t] * lax.rsqrt(pivots)
    whole = jnp.concatenate(slabs, axis=0)
    rows = lax.broadcasted_iota(jnp.int32, (n, n), 0)
    lanes = lax.broadcasted_iota(jnp.int32, (n, n), 1)
    return jnp.where(lanes <= rows, whole, 0.0)


def reciprocal(value):
    guess = pltpu.reciprocal(value, approx=True)
    return guess * (2.0 - value * guess)


def exchange_kernel(
    front_ref, tile_ref, child_ref, row_places_ref, col_places_ref,
    left_ref, right_ref, inverse_ref, child_out_ref,
    made, turned, early, corner, work, send_sems, left_sems, right_sems, inverse_sems,
    child_sems, corner_sems, local_sems,
):
    s = lax.axis_index("sub")
    r = lax.axis_index("row")
    c = lax.axis_index("col")
    z, h, k = c // 4, (c // 2) % 2, c % 2
    g = 4 * s + r

    def col_of(zz, hh, kk):
        return zz * 4 + hh * 2 + kk

    def at(ss=None, rr=None, cc=None):
        return (s if ss is None else ss, c if cc is None else cc, r if rr is None else rr)

    z_up, z_down = (z + 1) % 8, (z + 7) % 8
    to_up = at(cc=col_of(z_up, h, k))
    to_down = at(cc=col_of(z_down, h, k))
    to_far = at(cc=col_of(z, 1 - h, k))
    to_twin = at(cc=col_of(z, h, 1 - k))
    to_sub = at(ss=1 - s)

    def to_row(rr):
        return at(rr=rr)

    barrier = pltpu.get_barrier_semaphore()
    friends = [to_up, to_down, to_far, to_twin, to_sub]
    for step in (1, 2, 3):
        friends.append(at(rr=(r + step) % 4))
        friends.append(at(ss=1 - s, rr=(r + step) % 4))
        friends.append(at(rr=(r + step) % 4, cc=col_of(z, 1 - h, k)))
        friends.append(at(ss=1 - s, rr=(r + step) % 4, cc=col_of(z, 1 - h, k)))
    friends.append(at(ss=1 - s, cc=col_of(z, 1 - h, k)))
    for friend in friends:
        pl.semaphore_signal(barrier, inc=1, device_id=friend, device_id_type=MESH)
    pl.semaphore_wait(barrier, len(friends))

    pending = []
    used = [0]

    def slot():
        used[0] += 1
        return send_sems.at[used[0] - 1]

    def send(conditions, source, target, arrive, device):
        copy = pltpu.make_async_remote_copy(
            src_ref=source, dst_ref=target, send_sem=slot(), recv_sem=arrive,
            device_id=device, device_id_type=MESH,
        )
        condition = functools.reduce(jnp.logical_and, conditions)

        @pl.when(condition)
        def _():
            copy.start()

        pending.append((condition, copy))

    def await_at(target, arrive):
        pltpu.make_async_remote_copy(
            src_ref=target, dst_ref=target, send_sem=send_sems.at[0], recv_sem=arrive,
            device_id=to_twin, device_id_type=MESH,
        ).wait_recv()

    always = jnp.bool_(True)
    first = s == 0
    maker = jnp.logical_and(s == 0, r < 2)
    sender_early = jnp.logical_and(s == 1, r < 2)

    send(
        [sender_early],
        child_ref.at[0, pl.ds(0, TILE), :], early, child_sems.at[4], to_sub,
    )

    def send_children(numbers):
        for m in numbers:
            place = pl.multiple_of((2 * m + 1 - s) * TILE, TILE)
            send(
                [always],
                child_ref.at[0, pl.ds(place, TILE), :], child_out_ref.at[m],
                child_sems.at[m], to_sub,
            )

    send_children((0, 1))

    @pl.when(maker)
    def _():
        await_at(early, child_sems.at[4])
        total = front_ref[...]
        for source in range(2):
            tile = tile_ref[0] if source == 0 else early[...]
            total = total + permuted(
                tile,
                one_hot(row_places_ref[source : source + 1, :], TILE),
                one_hot(col_places_ref[source : source + 1, :], 2 * TILE),
            )
        made[...] = total.reshape(2, HALF, 2 * TILE)
        turned[...] = total.T

    own_left = c % 8 == g
    left_block = c // 8
    left_group = c % 8
    goal = at(ss=left_group // 4, rr=left_group % 4)
    far_goal = at(ss=left_group // 4, rr=left_group % 4, cc=col_of(z, 1 - h, k))
    local_copies = []

    def copy_here(conditions, source, target, number):
        copy = pltpu.make_async_copy(source, target, local_sems.at[number])
        condition = functools.reduce(jnp.logical_and, conditions)

        @pl.when(condition)
        def _():
            copy.start()

        local_copies.append((condition, copy))

    for part in range(2):
        send(
            [first, r == 0, c == 0],
            made.at[part, :, pl.ds(0, TILE)], corner.at[part], corner_sems.at[part],
            at(cc=1),
        )
        send(
            [first, r == 1, c == 1],
            made.at[part, :, pl.ds(0, TILE)], corner.at[2 + part], corner_sems.at[2 + part],
            to_row(0),
        )
    def left_at(m, q):
        return left_ref.at[m, q // PARTS, pl.ds(q % PARTS * RUN, RUN), :]

    for panel in range(2):
        here = [first, r == panel]
        for part in range(PARTS):
            q = PARTS * panel + part
            piece = turned.at[pl.ds(part * RUN, RUN), :]
            send(
                here + [jnp.logical_not(own_left)],
                piece, left_at(left_block, q), left_sems.at[left_block, q], goal,
            )
            send(here, piece, left_at(left_block, q), left_sems.at[left_block, q], far_goal)
        copy_here(here + [own_left], turned, left_ref.at[left_block, panel], panel)
        copy_here(here, made, right_ref.at[pl.ds(2 * panel, 2)], 4 + panel)
    for panel in range(2):
        for part in range(2):
            q = 2 * panel + part
            here = [first, r == panel]
            for target in (to_sub, to_row((panel + 1) % 4), to_row((panel + 3) % 4)):
                send(here, made.at[part], right_ref.at[q], right_sems.at[q], target)
    for condition, copy in local_copies:
        pl.when(condition)(copy.wait)

    rides = k == r % 2
    home = h == r // 2
    even = z % 2 == s
    source_rider = jnp.logical_and(rides, even)
    other_rider = jnp.logical_and(rides, jnp.logical_not(even))
    mine = (z // 2) % 4

    def await_left(conditions, m, q):
        condition = functools.reduce(jnp.logical_and, conditions)

        @pl.when(condition)
        def _():
            await_at(left_at(m, q), left_sems.at[m, q])

    def pass_left(conditions, m, q, devices):
        for device in devices:
            send(conditions, left_at(m, q), left_at(m, q), left_sems.at[m, q], device)

    not_made = [
        jnp.logical_not(jnp.logical_and(home, jnp.logical_and(first, r == panel)))
        for panel in range(2)
    ]
    order = [part + PARTS * panel for part in range(PARTS) for panel in range(2)]
    for q in order:
        await_left([source_rider, not_made[q // PARTS]], mine, q)
        pass_left([source_rider], mine, q, [to_up, to_down, to_twin])

    def pass_right(who):
        for panel in range(2):
            near, far, last = (panel + 1) % 4, (panel + 3) % 4, (panel + 2) % 4
            passer = far if panel == 0 else near
            for part in range(2):
                q = 2 * panel + part
                turn = jnp.logical_and(jnp.logical_not(first), r == panel)
                passes = jnp.logical_and(who, jnp.logical_or(turn, r == passer))

                @pl.when(passes)
                def _():
                    await_at(right_ref.at[q], right_sems.at[q])

                for condition, target in ((turn, near), (turn, far), (r == passer, last)):
                    send(
                        [who, condition],
                        right_ref.at[q], right_ref.at[q], right_sems.at[q], to_row(target),
                    )

    def await_right(who):
        for panel in range(2):
            passer = (panel + 3) % 4 if panel == 0 else (panel + 1) % 4
            for part in range(2):
                q = 2 * panel + part
                done = jnp.logical_or(r == panel, r == passer)

                @pl.when(jnp.logical_and(who, jnp.logical_not(done)))
                def _():
                    await_at(right_ref.at[q], right_sems.at[q])

    pass_right(jnp.logical_not(rides))

    chief = jnp.logical_and(jnp.logical_and(first, r == 0), c == 1)
    blocks = 2 * TILE // LEAF

    @pl.when(chief)
    def _():
        for part in range(4):
            await_at(corner.at[part], corner_sems.at[part])
        work[0:TILE, 0:TILE] = corner[0:2].reshape(TILE, TILE)
        work[0:TILE, TILE:] = made[:, :, 0:TILE].reshape(TILE, TILE)
        work[TILE:, TILE:] = corner[2:4].reshape(TILE, TILE)
        work[TILE:, 0:TILE] = jnp.zeros((TILE, TILE), F32)

    lanes = lax.broadcasted_iota(jnp.int32, (1, 2 * TILE), 1)
    w_children = [
        ([k == 1], to_twin),
        ([k == 1, r == 0], to_row(1)),
        ([k == 1, r == 0], to_row(3)),
        ([k == 1, r == 1], to_row(2)),
        ([k == 1, r == 0, first], to_sub),
        ([k == 1, r == 0, first, h == 0], to_far),
        ([k == 1, r == 0, first, h == 0, z <= 3], to_up),
        ([k == 1, r == 0, first, h == 0, jnp.logical_or(z == 0, z > 5)], to_down),
    ][::-1]

    def inverse_at(b):
        reach = ((b + 1) * LEAF + HALF - 1) // HALF * HALF
        return inverse_ref.at[b, :, pl.ds(0, reach)]

    def send_inverse(b, conditions):
        for more, device in w_children:
            send(
                conditions + more,
                inverse_at(b), inverse_at(b), inverse_sems.at[b], device,
            )

    for b in range(blocks):
        low, high = b * LEAF, (b + 1) * LEAF

        @pl.when(chief)
        def _():
            rows = work[low:high, :]
            leaf = leaf_inverse(rows[:, low:high])
            placed = jnp.concatenate(
                ([jnp.zeros((LEAF, low), F32)] if low else [])
                + [jnp.where(
                    lax.broadcasted_iota(jnp.int32, (LEAF, LEAF), 0)
                    == lax.broadcasted_iota(jnp.int32, (LEAF, LEAF), 1), 1.0, 0.0)]
                + ([jnp.zeros((LEAF, 2 * TILE - high), F32)] if high < 2 * TILE else []),
                axis=1,
            )
            in_block = jnp.logical_and(lanes >= low, lanes < high)
            rows = jnp.where(in_block, placed, rows)
            product = dot(leaf, rows, ((1,), (0,)), HIGHEST)
            made_inverse = jnp.where(lanes < high, product, 0.0)
            early_rows = made_inverse
            work[low:high, :] = early_rows
            if high < 2 * TILE:
                later = product[:, high:]
                below = jnp.where(in_block, 0.0, work[high:, :])
                work[high:, :] = below - dot(later, product, ((0,), (0,)), HIGHEST)
            copy = pltpu.make_async_copy(
                work.at[pl.ds(low, LEAF), :], inverse_ref.at[b], local_sems.at[12]
            )
            copy.start()
            copy.wait()

        send_inverse(b, [chief])

    above, below = (mine + 1) % 4, (mine + 3) % 4
    across = (mine + 2) % 4
    block_down = ((z + 7 - s) // 2) % 4
    block_up = ((z + 1 + 8 - s) // 2) % 4
    for q in order:
        await_left([other_rider], block_down, q)
        pass_left([other_rider], block_down, q, [to_up, to_twin])
        await_left([other_rider], block_up, q)
        pass_left([other_rider], block_up, q, [to_down, to_twin])
        await_left([source_rider], below, q)
        pass_left([source_rider], below, q, [to_up, to_twin])
        await_left([source_rider], above, q)
        pass_left([source_rider], above, q, [to_down, to_twin])
    pass_right(rides)
    send_children((2, 3))
    far_down, far_up = (block_down + 3) % 4, (block_up + 1) % 4
    for q in order:
        await_left([other_rider], far_down, q)
        pass_left([other_rider], far_down, q, ([to_up] if q < PARTS else []) + [to_twin])
        await_left([other_rider], far_up, q)
        pass_left([other_rider], far_up, q, ([to_down] if q >= PARTS else []) + [to_twin])
        await_left([source_rider], across, q)
        pass_left([source_rider], across, q, [to_twin])

    for b in range(blocks):
        @pl.when(jnp.logical_not(chief))
        def _():
            await_at(inverse_at(b), inverse_sems.at[b])

        send_inverse(b, [jnp.logical_not(chief)])

    await_right(always)
    for m in range(4):
        for q in range(2 * PARTS):
            await_left([jnp.logical_not(rides)], m, q)
    for m in range(4):
        await_at(child_out_ref.at[m], child_sems.at[m])
    for condition, copy in pending:
        pl.when(condition)(copy.wait_send)


SENDS = 400


def exchange(front_in, child_update, row_places, col_places):
    blocks = 2 * TILE // LEAF
    outs = (
        jax.ShapeDtypeStruct((4, 2, 2 * TILE, TILE), F32),
        jax.ShapeDtypeStruct((4, HALF, 2 * TILE), F32),
        jax.ShapeDtypeStruct((blocks, LEAF, 2 * TILE), F32),
        jax.ShapeDtypeStruct((4, TILE, TILE), F32),
    )
    return pl.pallas_call(
        exchange_kernel,
        out_shape=outs,
        grid=(1,),
        in_specs=[
            pl.BlockSpec((TILE, 2 * TILE), lambda i: (0, 0)),
            pl.BlockSpec((1, TILE, TILE), lambda i: (0, 0, 0)),
            pl.BlockSpec(memory_space=pl.ANY),
            pl.BlockSpec((2, TILE), lambda i: (0, 0)),
            pl.BlockSpec((2, TILE), lambda i: (0, 0)),
        ],
        out_specs=[pl.BlockSpec(memory_space=pl.ANY)] * 4,
        scratch_shapes=[
            pltpu.VMEM((2, HALF, 2 * TILE), F32),
            pltpu.VMEM((2 * TILE, TILE), F32),
            pltpu.VMEM((TILE, TILE), F32),
            pltpu.VMEM((4, HALF, TILE), F32),
            pltpu.VMEM((2 * TILE, 2 * TILE), F32),
            pltpu.SemaphoreType.DMA((SENDS,)),
            pltpu.SemaphoreType.DMA((4, 2 * PARTS)),
            pltpu.SemaphoreType.DMA((4,)),
            pltpu.SemaphoreType.DMA((blocks,)),
            pltpu.SemaphoreType.DMA((5,)),
            pltpu.SemaphoreType.DMA((4,)),
            pltpu.SemaphoreType.DMA((13,)),
        ],
        compiler_params=pltpu.CompilerParams(
            collective_id=0, has_side_effects=True, vmem_limit_bytes=48 * 1024 * 1024
        ),
        name="exchange",
    )(front_in, child_update, child_update, row_places, col_places)


def update_kernel(
    facts_ref, front_ref, mine_ref, other_ref, row_places_ref, col_places_ref,
    left_ref, right_ref, inverse_ref, out_ref, w_high, w_low, right_high, right_low,
):
    m = pl.program_id(0)
    s, r, c = facts_ref[0], facts_ref[1], facts_ref[2]
    g = 4 * s + r
    nn, nt = ((1,), (0,)), ((1,), (1,))

    def half_of(ref_high, ref_low, row, col):
        rows, cols = pl.ds(row * TILE, TILE), pl.ds(col * TILE, TILE)
        return ref_high[rows, cols], ref_low[rows, cols]

    @pl.when(m == 0)
    def _():
        rows = lax.broadcasted_iota(jnp.int32, (2 * TILE, 2 * TILE), 0)
        lanes = lax.broadcasted_iota(jnp.int32, (2 * TILE, 2 * TILE), 1)
        inverse = inverse_ref[...].reshape(2 * TILE, 2 * TILE)
        w_high[...], w_low[...] = split2(jnp.where(lanes <= rows, inverse, 0.0))
        high, low = split2(right_ref[...].reshape(2 * TILE, 2 * TILE))
        upper = dot3(half_of(w_high, w_low, 0, 0), (high[:TILE], low[:TILE]), nn)
        lower = dot3((w_high[TILE:], w_low[TILE:]), (high, low), nn)
        right_high[:TILE], right_low[:TILE] = split2(upper)
        right_high[TILE:], right_low[TILE:] = split2(lower)

    first, second = split2(left_ref[0, 0]), split2(left_ref[0, 1])
    done = (
        dot3(first, half_of(w_high, w_low, 0, 0), nt),
        dot3(first, half_of(w_high, w_low, 1, 0), nt)
        + dot3(second, half_of(w_high, w_low, 1, 1), nt),
    )
    total = None
    for part in range(2):
        rows = pl.ds(part * TILE, TILE)
        product = dot3(split2(done[part]), (right_high[rows, :], right_low[rows, :]), nn)
        total = product if total is None else total + product
    for half in range(2):
        out_ref[half, 0] = front_ref[half, 0] - total[half * TILE : (half + 1) * TILE]
    for source in range(2):
        tile = jnp.where(s == source, mine_ref[0], other_ref[0])
        moved = permuted(
            tile,
            one_hot(row_places_ref[0, source : source + 1, :], TILE),
            one_hot(col_places_ref[source : source + 1, :], TILE),
        )
        half = facts_ref[4 + 4 * source + m]
        place = pl.multiple_of(facts_ref[12 + source] * TILE, TILE)
        out_ref[half, 0, :, pl.ds(place, TILE)] += moved

    @pl.when(c < 2)
    def _():
        rows = lax.broadcasted_iota(jnp.int32, (TILE, TILE), 0)
        lanes = lax.broadcasted_iota(jnp.int32, (TILE, TILE), 1)
        for half in range(2):
            number = g + 8 * m + 32 * half
            cut = slice(half * TILE, (half + 1) * TILE)
            panel = jnp.where(c == 0, done[0][cut], done[1][cut])
            keep = jnp.logical_or(number > c, jnp.logical_and(number == c, lanes <= rows))
            out_ref[half, 0, :, 0:TILE] = jnp.where(keep, panel, 0.0)

    @pl.when(jnp.logical_and(m == 0, g < 2))
    def _():
        out_ref[0, 0, :, TILE:] = jnp.zeros((TILE, TILE), F32)

    @pl.when(jnp.logical_and(jnp.logical_and(m == 0, g < 2), c >= 2))
    def _():
        out_ref[0, 0, :, 0:TILE] = jnp.zeros((TILE, TILE), F32)


def update(facts, front_in, child_update, arrived, row_places, col_places, left, right, inverse):
    blocks = 2 * TILE // LEAF
    grid_spec = pltpu.PrefetchScalarGridSpec(
        num_scalar_prefetch=1,
        grid=(4,),
        in_specs=[
            pl.BlockSpec((2, 1, TILE, 2 * TILE), lambda m, f: (0, m, 0, 0)),
            pl.BlockSpec((1, TILE, TILE), lambda m, f: (0, f[0] + 2 * m, 0)),
            pl.BlockSpec((1, TILE, TILE), lambda m, f: (m, 0, 0)),
            pl.BlockSpec((1, 2, TILE), lambda m, f: (m, 0, 0)),
            pl.BlockSpec((2, TILE), lambda m, f: (0, 0)),
            pl.BlockSpec((1, 2, 2 * TILE, TILE), lambda m, f: (m, 0, 0, 0)),
            pl.BlockSpec((4, HALF, 2 * TILE), lambda m, f: (0, 0, 0)),
            pl.BlockSpec((blocks, LEAF, 2 * TILE), lambda m, f: (0, 0, 0)),
        ],
        out_specs=pl.BlockSpec((2, 1, TILE, 2 * TILE), lambda m, f: (0, m, 0, 0)),
        scratch_shapes=[pltpu.VMEM((2 * TILE, 2 * TILE), BF16)] * 4,
    )
    out = pl.pallas_call(
        update_kernel,
        out_shape=jax.ShapeDtypeStruct((2, 4, TILE, 2 * TILE), F32),
        grid_spec=grid_spec,
        compiler_params=pltpu.CompilerParams(vmem_limit_bytes=48 * 1024 * 1024),
        name="update",
    )(
        facts, front_in.reshape(2, 4, TILE, 2 * TILE), child_update, arrived,
        row_places, col_places, left, right, inverse,
    )
    return out.reshape(8 * TILE, 2 * TILE)


def local(front_in, child_update, child_map):
    s = lax.axis_index("sub")
    r = lax.axis_index("row")
    c = lax.axis_index("col")
    g = 4 * s + r
    tiles = child_map.reshape(2, 32, TILE)
    col_map = lax.dynamic_index_in_dim(tiles, c, 1, keepdims=False)
    row_map = lax.dynamic_index_in_dim(tiles.reshape(2, 4, 8, TILE), g, 2, keepdims=False)
    early_rows = row_map[:, 0] - g * TILE
    early_cols = col_map // (32 * TILE) * TILE + col_map % TILE
    left, right, inverse, arrived = exchange(front_in, child_update, early_rows, early_cols)
    facts = jnp.concatenate(
        [
            jnp.stack([s, r, c, 0 * s]).astype(jnp.int32),
            (row_map[:, :, 0] // (32 * TILE)).reshape(-1),
            col_map[:, 0] // (32 * TILE),
        ]
    )
    return update(
        facts, front_in, child_update, arrived,
        jnp.swapaxes(row_map % TILE, 0, 1), col_map % TILE, left, right, inverse,
    )


def solution(mesh):
    placed = (P(("sub", "row"), "col"), P("sub", "row", "col"), P())
    return jax.shard_map(
        local, mesh=mesh, in_specs=placed, out_specs=P(("sub", "row"), "col"), check_vma=False
    )
```
